32 devices in a mesh: groups: 2 (over x), gx: 16 (over z, y, core).
Axes of the slice: x: 2, y: 2, z: 4, core: 2. Of those that a mesh axis runs over, the one named last changes fastest.
Arguments:
- cotangent: float32 [16, 2048, 2048], P('groups', 'gx'), parts along dimension 0, may hold values from -6 to 6
- saved_v: float32 [16, 2048, 2048], P('groups', 'gx'), parts along dimension 0, may hold values from 0.3 to 3
- saved_u: float32 [16, 2048, 2048], P('groups', None, 'gx'), parts along dimension 0, may hold values from 0.3 to 3
- gain_x: float32 [2048], replicated, may hold values from 0.1 to 1.9
- width_x: int32 [2048], replicated, may hold values from 16 to 256
- gain_y: float32 [2048], replicated, may hold values from 0.1 to 1.9
- width_y: int32 [2048], replicated, may hold values from 16 to 256
Outputs:
- grad_u: float32 [16, 2048, 2048], P('groups', None, 'gx'), parts along dimension 0
- grad_v: float32 [16, 2048, 2048], P('groups', 'gx'), parts along dimension 0
The draws below stay inside these ranges and needn't reach their ends.
There are 2 independent parts, one for each index of `groups`. The reference program is written for one: setup_inputs(seed, part) draws one part's arguments, and reference() takes and returns one part's arrays. A program takes and returns all parts, laid end to end along the dimension named above; an argument that names none is the same for every part. Nothing has to cross between parts.
All inputs are finite; a program needn't handle non-finite values.
Results may differ from the reference program's by a relative error of at most 0.00007.
Values sent between devices are 32-bit elements; how exact they have to be, the bound alone decides.
A program may use at most 192 MiB of HBM per device.

```python
import math
import jax
import jax.numpy as jnp
from jax import lax

X = 2048
Y = 2048
Z = 8
SIGMA = 64


def set_ends(result, own_key, low, top_value):
    dims = result.shape
    index_at = [jax.random.randint(jax.random.fold_in(own_key, axis), (), 0, dims[axis]) for axis in range(len(dims))]
    result = result.at[tuple(index_at)].set(low)
    longest = dims.index(max(dims))
    index_at[longest] = (index_at[longest] + 1) % dims[longest]
    return result.at[tuple(index_at)].set(top_value)


def shard_levels(rng, extent, shards, least, high):
    def one(position, blocks):
        heights = jax.random.uniform(jax.random.fold_in(jax.random.fold_in(rng, 6), position), (blocks,), jnp.float32, least / len(shards), high / len(shards))
        return jnp.repeat(jnp.exp(heights), extent[position] // blocks).reshape((-1,) + (1,) * (len(extent) - position - 1))

    factor_of = one(*shards[0])
    for cut in shards[1:]:
        factor_of = factor_of * one(*cut)
    return factor_of


def gaussian(own_key, dims, spread, most, cuts=(), held_as=jnp.bfloat16):
    level = shard_levels(own_key, dims, cuts, -0.22, 0.18) if cuts else 1.0
    result = jax.random.normal(own_key, dims, jnp.float32) * spread * level
    return jnp.minimum(jnp.maximum(result, -most), most).astype(held_as)


def setup_inputs(seed: int = 0, part: int = 0) -> dict:
    keys = jax.random.split(jax.random.key(seed), 8)
    part_keys = jax.random.split(jax.random.fold_in(keys[7], part), 8)
    return {
        "cotangent": gaussian(part_keys[0], (Z, X, Y), 1.0, 6.0, ((1, 16),), jnp.float32),
        "saved_v": jnp.clip(jnp.exp(math.log(3.0) - 2.3025851 * jax.random.uniform(part_keys[1], (Z, X, Y), jnp.float32) ** shard_levels(part_keys[1], (Z, X, Y), ((1, 16),), -0.2, 0.2)), 0.3, 3.0),
        "saved_u": jnp.clip(jnp.exp(math.log(3.0) - 2.3025851 * jax.random.uniform(part_keys[2], (Z, X, Y), jnp.float32) ** shard_levels(part_keys[2], (Z, X, Y), ((2, 16),), -0.2, 0.2)), 0.3, 3.0),
        "gain_x": jnp.clip(1.0 + 0.18 * jax.random.normal(keys[3], (X,), jnp.float32), 0.1, 1.9),
        "width_x": set_ends(jax.random.randint(keys[4], (X,), SIGMA // 4, 4 * SIGMA + 1), jax.random.fold_in(keys[4], 1), SIGMA // 4, 4 * SIGMA).astype(jnp.int32),
        "gain_y": jnp.clip(1.0 + 0.18 * jax.random.normal(keys[5], (Y,), jnp.float32), 0.1, 1.9),
        "width_y": set_ends(jax.random.randint(keys[6], (Y,), SIGMA // 4, 4 * SIGMA + 1), jax.random.fold_in(keys[6], 1), SIGMA // 4, 4 * SIGMA).astype(jnp.int32),
    }


def build_kernel(gain, width, count):
    rows = jnp.arange(count, dtype=jnp.int32)[:, None]
    cols = jnp.arange(count, dtype=jnp.int32)[None, :]
    offset = (rows - cols).astype(jnp.float32)
    scale = 1.0 / math.sqrt(SIGMA * math.sqrt(math.pi))
    values = gain[:, None] * jnp.exp(-offset * offset / (2.0 * SIGMA * SIGMA)) * scale
    cutoff = jnp.minimum(width[:, None], width[None, :])
    return jnp.where(jnp.abs(rows - cols) <= cutoff, values, jnp.zeros_like(values))

def reference(cotangent, saved_v, saved_u, gain_x, width_x, gain_y, width_y):
    kernel_x = build_kernel(gain_x, width_x, X)
    kernel_y = build_kernel(gain_y, width_y, Y)
    high = lax.Precision.HIGHEST
    weighted = saved_v * cotangent
    along_y = jnp.einsum('zxi,ij->zxj', weighted, kernel_y, precision=high)
    middle = jnp.einsum('ziy,ij->zjy', along_y, kernel_x, precision=high)
    grad_u = saved_u * middle
    back_x = jnp.einsum('ziy,ij->zjy', grad_u, kernel_x, precision=high)
    grad_v = jnp.einsum('zxi,ij->zxj', back_x, kernel_y, precision=high)
    return (grad_u, grad_v)
```

```python
import functools
import math

import jax
import jax.numpy as jnp
from jax import lax
from jax.experimental import pallas as pl
from jax.experimental.pallas import tpu as pltpu
from jax.sharding import PartitionSpec as P

SIGMA = 64
REACH = 256
TILE = 256
BAND = TILE + 2 * REACH
SCALE = 1.0 / math.sqrt(SIGMA * math.sqrt(math.pi))
MESH = pl.DeviceIdType.MESH


def build_kernel(gain, width, count):
    rows = jnp.arange(count, dtype=jnp.int32)[:, None]
    cols = jnp.arange(count, dtype=jnp.int32)[None, :]
    offset = (rows - cols).astype(jnp.float32)
    values = gain[:, None] * jnp.exp(-offset * offset / (2.0 * SIGMA * SIGMA)) * SCALE
    cutoff = jnp.minimum(width[:, None], width[None, :])
    return jnp.where(jnp.abs(rows - cols) <= cutoff, values, jnp.zeros_like(values))


def plain_form(cotangent, saved_v, saved_u, gain_x, width_x, gain_y, width_y):
    kernel_x = build_kernel(gain_x, width_x, gain_x.shape[0])
    kernel_y = build_kernel(gain_y, width_y, gain_y.shape[0])
    high = lax.Precision.HIGHEST

    def smooth_x(field):
        return jnp.einsum("ziy,ij->zjy", field, kernel_x, precision=high)

    def smooth_y(field):
        return jnp.einsum("zxi,ij->zxj", field, kernel_y, precision=high)

    weighted = saved_v * cotangent
    along_y = smooth_y(weighted)
    middle = smooth_x(lax.all_to_all(along_y, "gx", split_axis=2, concat_axis=1, tiled=True))
    grad_u = saved_u * middle
    back_x = smooth_x(grad_u)
    grad_v = smooth_y(lax.all_to_all(back_x, "gx", split_axis=1, concat_axis=2, tiled=True))
    return (grad_u, grad_v)


def parts_of(value):
    high = value.astype(jnp.bfloat16)
    return high, (value - high.astype(jnp.float32)).astype(jnp.bfloat16)


def dot(a, b):
    return jnp.dot(a, b, preferred_element_type=jnp.float32)


def three(a_hi, a_lo, b_hi, b_lo):
    return dot(a_hi, b_hi) + dot(a_hi, b_lo) + dot(a_lo, b_hi)


def fused(n, cot, sv, su, rows, cols, gu, gv,
          send_a, recv_a, send_b, recv_b, sv_buf, ky_hi, ky_lo, kx_hi, kx_lo,
          wide_hi, wide_lo, tall_hi, tall_lo,
          cot_sem, sv_sem, su_sem, gu_sem, gv_sem, sa_sem, ra_sem, sb_sem, rb_sem):
    count, mine_x, size_y = cot.shape
    size_x, mine_y = su.shape[1], su.shape[2]
    tiles_x, tiles_y = size_x // TILE, size_y // TILE
    me = lax.axis_index("gx")
    my_x = pl.multiple_of(me * mine_x, mine_x)
    my_y = pl.multiple_of(me * mine_y, mine_y)

    def load_cot(c):
        return pltpu.make_async_copy(cot.at[c], send_a.at[c], cot_sem.at[c])

    def load_sv(c):
        return pltpu.make_async_copy(sv.at[c], sv_buf.at[lax.rem(c, 2)], sv_sem.at[c])

    def load_su(c):
        return pltpu.make_async_copy(su.at[c], send_b.at[c], su_sem.at[c])

    def store_gu(c):
        return pltpu.make_async_copy(recv_a.at[c], gu.at[c], gu_sem.at[c])

    def store_gv(c):
        return pltpu.make_async_copy(send_a.at[c], gv.at[c], gv_sem.at[c])

    for c in range(count):
        load_cot(c).start()
        if c < 2:
            load_sv(c).start()

    barrier = pltpu.get_barrier_semaphore()
    for k in range(1, n):
        pl.semaphore_signal(barrier, inc=1, device_id={"gx": lax.rem(me + k, n)}, device_id_type=MESH)

    def band_start(t, size):
        return pl.multiple_of(jnp.clip(t * TILE - REACH, 0, size - BAND), TILE)

    def values(i, j, gain, width_i, width_j):
        offset = (i - j).astype(jnp.float32)
        cell = gain * jnp.exp(-offset * offset / (2.0 * SIGMA * SIGMA)) * SCALE
        return jnp.where(jnp.abs(offset) <= jnp.minimum(width_i, width_j), cell, 0.0)

    def build_y(t, _):
        i0, j0 = band_start(t, size_y), pl.multiple_of(t * TILE, TILE)
        j = j0 + lax.broadcasted_iota(jnp.int32, (TILE, TILE), 1)
        for s in range(BAND // TILE):
            at = pl.multiple_of(i0 + s * TILE, TILE)
            i = at + lax.broadcasted_iota(jnp.int32, (TILE, TILE), 0)
            hi, lo = parts_of(values(i, j, cols[pl.ds(at, TILE), 2:3], cols[pl.ds(at, TILE), 3:4],
                                     rows[3:4, pl.ds(j0, TILE)]))
            ky_hi[t, s * TILE:(s + 1) * TILE, :] = hi
            ky_lo[t, s * TILE:(s + 1) * TILE, :] = lo
        return 0

    def build_x(t, _):
        i0, j0 = band_start(t, size_x), pl.multiple_of(t * TILE, TILE)
        j = j0 + lax.broadcasted_iota(jnp.int32, (TILE, TILE), 0)
        for s in range(BAND // TILE):
            at = pl.multiple_of(i0 + s * TILE, TILE)
            i = at + lax.broadcasted_iota(jnp.int32, (TILE, TILE), 1)
            hi, lo = parts_of(values(i, j, rows[0:1, pl.ds(at, TILE)], rows[1:2, pl.ds(at, TILE)],
                                     cols[pl.ds(j0, TILE), 1:2]))
            kx_hi[t, :, s * TILE:(s + 1) * TILE] = hi
            kx_lo[t, :, s * TILE:(s + 1) * TILE] = lo
        return 0

    def smooth_y(c):
        def tile(t, _):
            band = pl.ds(band_start(t, size_y), BAND)
            send_a[c, :, pl.ds(pl.multiple_of(t * TILE, TILE), TILE)] = three(
                wide_hi[:, band], wide_lo[:, band], ky_hi[t], ky_lo[t])
            return 0
        lax.fori_loop(0, tiles_y, tile, 0)

    def smooth_x(t):
        band = pl.ds(band_start(t, size_x), BAND)
        return three(kx_hi[t], kx_lo[t], tall_hi[band, :], tall_lo[band, :])

    lax.fori_loop(0, tiles_y, build_y, 0)
    pl.semaphore_wait(barrier, n - 1)

    def first(c, _):
        load_cot(c).wait()
        load_sv(c).wait()
        hi, lo = parts_of(send_a[c] * sv_buf[lax.rem(c, 2)])
        wide_hi[...] = hi
        wide_lo[...] = lo

        @pl.when(c + 2 < count)
        def _():
            load_sv(c + 2).start()

        smooth_y(c)
        for k in range(1, n):
            p = lax.rem(me + k, n)
            pltpu.make_async_remote_copy(
                src_ref=send_a.at[c, :, pl.ds(pl.multiple_of(p * mine_y, mine_y), mine_y)],
                dst_ref=recv_a.at[c, pl.ds(my_x, mine_x), :],
                send_sem=sa_sem.at[c], recv_sem=ra_sem.at[c],
                device_id={"gx": p}, device_id_type=MESH).start()
        recv_a[c, pl.ds(my_x, mine_x), :] = send_a[c, :, pl.ds(my_y, mine_y)]
        load_su(c).start()
        return 0

    lax.fori_loop(0, count, first, 0)
    lax.fori_loop(0, tiles_x, build_x, 0)

    def tall_part(ref, c, sem):
        part = ref.at[c, pl.ds(0, size_x - mine_x), :]
        return pltpu.make_async_copy(part, part, sem.at[c])

    def wide_part(ref, c, sem):
        part = ref.at[c, :, pl.ds(0, size_y - mine_y)]
        return pltpu.make_async_copy(part, part, sem.at[c])

    def second(c, _):
        tall_part(recv_a, c, ra_sem).wait()
        hi, lo = parts_of(recv_a[c])
        tall_hi[...] = hi
        tall_lo[...] = lo
        load_su(c).wait()

        def up(t, _):
            out = pl.ds(pl.multiple_of(t * TILE, TILE), TILE)
            recv_a[c, out, :] = send_b[c, out, :] * smooth_x(t)
            return 0

        lax.fori_loop(0, tiles_x, up, 0)
        store_gu(c).start()
        hi, lo = parts_of(recv_a[c])
        tall_hi[...] = hi
        tall_lo[...] = lo

        def back(t, _):
            send_b[c, pl.ds(pl.multiple_of(t * TILE, TILE), TILE), :] = smooth_x(t)
            return 0

        lax.fori_loop(0, tiles_x, back, 0)
        for k in range(1, n):
            p = lax.rem(me + k, n)
            pltpu.make_async_remote_copy(
                src_ref=send_b.at[c, pl.ds(pl.multiple_of(p * mine_x, mine_x), mine_x), :],
                dst_ref=recv_b.at[c, :, pl.ds(my_y, mine_y)],
                send_sem=sb_sem.at[c], recv_sem=rb_sem.at[c],
                device_id={"gx": p}, device_id_type=MESH).start()
        recv_b[c, :, pl.ds(my_y, mine_y)] = send_b[c, pl.ds(my_x, mine_x), :]
        return 0

    lax.fori_loop(0, count, second, 0)

    def third(c, _):
        wide_part(send_a, c, sa_sem).wait()
        wide_part(recv_b, c, rb_sem).wait()
        hi, lo = parts_of(recv_b[c])
        wide_hi[...] = hi
        wide_lo[...] = lo
        smooth_y(c)
        store_gv(c).start()
        return 0

    lax.fori_loop(0, count, third, 0)

    def finish(c, _):
        tall_part(send_b, c, sb_sem).wait()
        store_gu(c).wait()
        store_gv(c).wait()
        return 0

    lax.fori_loop(0, count, finish, 0)


def kernel_form(n, cotangent, saved_v, saved_u, gain_x, width_x, gain_y, width_y):
    count, mine_x, size_y = cotangent.shape
    size_x, mine_y = saved_u.shape[1:]
    rows = jnp.stack([gain_x, width_x.astype(jnp.float32), gain_y, width_y.astype(jnp.float32)])
    f32, bf16 = jnp.float32, jnp.bfloat16
    work = 12 * 2 * count * BAND * (mine_x * size_y + mine_y * size_x)
    return pl.pallas_call(
        functools.partial(fused, n),
        out_shape=(jax.ShapeDtypeStruct(saved_u.shape, f32), jax.ShapeDtypeStruct(cotangent.shape, f32)),
        in_specs=[pl.BlockSpec(memory_space=pl.ANY)] * 3 + [pl.BlockSpec(memory_space=pltpu.VMEM)] * 2,
        out_specs=(pl.BlockSpec(memory_space=pl.ANY),) * 2,
        scratch_shapes=[
            pltpu.VMEM((count, mine_x, size_y), f32),
            pltpu.VMEM((count, size_x, mine_y), f32),
            pltpu.VMEM((count, size_x, mine_y), f32),
            pltpu.VMEM((count, mine_x, size_y), f32),
            pltpu.VMEM((2, mine_x, size_y), f32),
            pltpu.VMEM((size_y // TILE, BAND, TILE), bf16),
            pltpu.VMEM((size_y // TILE, BAND, TILE), bf16),
            pltpu.VMEM((size_x // TILE, TILE, BAND), bf16),
            pltpu.VMEM((size_x // TILE, TILE, BAND), bf16),
            pltpu.VMEM((mine_x, size_y), bf16),
            pltpu.VMEM((mine_x, size_y), bf16),
            pltpu.VMEM((size_x, mine_y), bf16),
            pltpu.VMEM((size_x, mine_y), bf16),
        ] + [pltpu.SemaphoreType.DMA((count,))] * 9,
        compiler_params=pltpu.CompilerParams(
            collective_id=0, has_side_effects=True, vmem_limit_bytes=60 * 2**20),
        cost_estimate=pl.CostEstimate(
            flops=work, bytes_accessed=20 * cotangent.size, transcendentals=0),
    )(cotangent, saved_v, saved_u, rows, rows.T)


def on_device(n, *arrays):
    size_y, (size_x, mine_y), mine_x = arrays[0].shape[2], arrays[2].shape[1:], arrays[0].shape[1]
    fits = (size_x % TILE == 0 and size_y % TILE == 0 and min(size_x, size_y) >= BAND
            and mine_x % 128 == 0 and mine_y % 128 == 0 and n > 1)
    return kernel_form(n, *arrays) if fits else plain_form(*arrays)


def solution(mesh):
    in_specs = (
        P("groups", "gx", None),
        P("groups", "gx", None),
        P("groups", None, "gx"),
        P(),
        P(),
        P(),
        P(),
    )
    out_specs = (P("groups", None, "gx"), P("groups", "gx", None))
    return jax.shard_map(
        functools.partial(on_device, mesh.shape["gx"]),
        mesh=mesh, in_specs=in_specs, out_specs=out_specs, check_vma=False
    )
```

```python
import functools
import math

import jax
import jax.numpy as jnp
from jax import lax
from jax.experimental import pallas as pl
from jax.experimental.pallas import tpu as pltpu
from jax.sharding import PartitionSpec as P

SIGMA = 64
REACH = 256
TILE = 256
BAND = TILE + 2 * REACH
SCALE = 1.0 / math.sqrt(SIGMA * math.sqrt(math.pi))
MESH = pl.DeviceIdType.MESH


def build_kernel(gain, width, count):
    rows = jnp.arange(count, dtype=jnp.int32)[:, None]
    cols = jnp.arange(count, dtype=jnp.int32)[None, :]
    offset = (rows - cols).astype(jnp.float32)
    values = gain[:, None] * jnp.exp(-offset * offset / (2.0 * SIGMA * SIGMA)) * SCALE
    cutoff = jnp.minimum(width[:, None], width[None, :])
    return jnp.where(jnp.abs(rows - cols) <= cutoff, values, jnp.zeros_like(values))


def plain_form(cotangent, saved_v, saved_u, gain_x, width_x, gain_y, width_y):
    kernel_x = build_kernel(gain_x, width_x, gain_x.shape[0])
    kernel_y = build_kernel(gain_y, width_y, gain_y.shape[0])
    high = lax.Precision.HIGHEST

    def smooth_x(field):
        return jnp.einsum("ziy,ij->zjy", field, kernel_x, precision=high)

    def smooth_y(field):
        return jnp.einsum("zxi,ij->zxj", field, kernel_y, precision=high)

    weighted = saved_v * cotangent
    along_y = smooth_y(weighted)
    middle = smooth_x(lax.all_to_all(along_y, "gx", split_axis=2, concat_axis=1, tiled=True))
    grad_u = saved_u * middle
    back_x = smooth_x(grad_u)
    grad_v = smooth_y(lax.all_to_all(back_x, "gx", split_axis=1, concat_axis=2, tiled=True))
    return (grad_u, grad_v)


def parts_of(value):
    high = value.astype(jnp.bfloat16)
    return high, (value - high.astype(jnp.float32)).astype(jnp.bfloat16)


def dot(a, b):
    return jnp.dot(a, b, preferred_element_type=jnp.float32)


def three(a_hi, a_lo, b_hi, b_lo):
    return dot(a_hi, b_hi) + dot(a_hi, b_lo) + dot(a_lo, b_hi)


def fused(n, cot, sv, su, rows, cols, recv_a, send_a,
          send_b, recv_b, sv_buf, ky_hi, ky_lo, kx_hi, kx_lo,
          wide_hi, wide_lo, tall_hi, tall_lo,
          cot_sem, sv_sem, su_sem, sa_sem, ra_sem, sb_sem, rb_sem):
    count, mine_x, size_y = cot.shape
    size_x, mine_y = su.shape[1], su.shape[2]
    tiles_x, tiles_y = size_x // TILE, size_y // TILE
    me = lax.axis_index("gx")
    my_x = pl.multiple_of(me * mine_x, mine_x)
    my_y = pl.multiple_of(me * mine_y, mine_y)

    def load_cot(c):
        return pltpu.make_async_copy(cot.at[c], send_a.at[c], cot_sem.at[c])

    def load_sv(c):
        return pltpu.make_async_copy(sv.at[c], sv_buf.at[lax.rem(c, 2)], sv_sem.at[c])

    def load_su(c):
        return pltpu.make_async_copy(su.at[c], send_b.at[c], su_sem.at[c])

    for c in range(count):
        load_cot(c).start()
        if c < 2:
            load_sv(c).start()

    barrier = pltpu.get_barrier_semaphore()
    for k in range(1, n):
        pl.semaphore_signal(barrier, inc=1, device_id={"gx": lax.rem(me + k, n)}, device_id_type=MESH)

    def turn(s, tiles, mine):
        half = tiles // 2
        away = jnp.where(lax.rem(s, 2) == 0, half + s // 2, lax.rem((s + 1) // 2, half))
        return lax.rem(my_tile(mine) + away, tiles)

    def my_tile(mine):
        return me // (TILE // mine)

    def band_start(t, size):
        return pl.multiple_of(jnp.clip(t * TILE - REACH, 0, size - BAND), TILE)

    def values(i, j, gain, width_i, width_j):
        offset = (i - j).astype(jnp.float32)
        cell = gain * jnp.exp(-offset * offset / (2.0 * SIGMA * SIGMA)) * SCALE
        return jnp.where(jnp.abs(offset) <= jnp.minimum(width_i, width_j), cell, 0.0)

    def build_y(t, _):
        i0, j0 = band_start(t, size_y), pl.multiple_of(t * TILE, TILE)
        j = j0 + lax.broadcasted_iota(jnp.int32, (TILE, TILE), 1)
        for s in range(BAND // TILE):
            at = pl.multiple_of(i0 + s * TILE, TILE)
            i = at + lax.broadcasted_iota(jnp.int32, (TILE, TILE), 0)
            hi, lo = parts_of(values(i, j, cols[pl.ds(at, TILE), 2:3], cols[pl.ds(at, TILE), 3:4],
                                     rows[3:4, pl.ds(j0, TILE)]))
            ky_hi[t, s * TILE:(s + 1) * TILE, :] = hi
            ky_lo[t, s * TILE:(s + 1) * TILE, :] = lo
        return 0

    def build_x(t, _):
        i0, j0 = band_start(t, size_x), pl.multiple_of(t * TILE, TILE)
        j = j0 + lax.broadcasted_iota(jnp.int32, (TILE, TILE), 0)
        for s in range(BAND // TILE):
            at = pl.multiple_of(i0 + s * TILE, TILE)
            i = at + lax.broadcasted_iota(jnp.int32, (TILE, TILE), 1)
            hi, lo = parts_of(values(i, j, rows[0:1, pl.ds(at, TILE)], rows[1:2, pl.ds(at, TILE)],
                                     cols[pl.ds(j0, TILE), 1:2]))
            kx_hi[t, :, s * TILE:(s + 1) * TILE] = hi
            kx_lo[t, :, s * TILE:(s + 1) * TILE] = lo
        return 0

    def smooth_y(c, t):
        band = pl.ds(band_start(t, size_y), BAND)
        send_a[c, :, pl.ds(pl.multiple_of(t * TILE, TILE), TILE)] = three(
            wide_hi[:, band], wide_lo[:, band], ky_hi[t], ky_lo[t])

    def smooth_x(t):
        band = pl.ds(band_start(t, size_x), BAND)
        return three(kx_hi[t], kx_lo[t], tall_hi[band, :], tall_lo[band, :])

    pl.semaphore_wait(barrier, n - 1)

    def first(c, _):
        load_cot(c).wait()
        load_sv(c).wait()
        hi, lo = parts_of(send_a[c] * sv_buf[lax.rem(c, 2)])
        wide_hi[...] = hi
        wide_lo[...] = lo

        @pl.when(c + 2 < count)
        def _():
            load_sv(c + 2).start()

        def tile(s, _):
            t = turn(s, tiles_y, mine_y)

            @pl.when(c == 0)
            def _():
                build_y(t, 0)

            smooth_y(c, t)
            for k in range(TILE // mine_y):
                p = t * (TILE // mine_y) + k

                @pl.when(p != me)
                def _():
                    pltpu.make_async_remote_copy(
                        src_ref=send_a.at[c, :, pl.ds(pl.multiple_of(p * mine_y, mine_y), mine_y)],
                        dst_ref=recv_a.at[c, pl.ds(my_x, mine_x), :],
                        send_sem=sa_sem.at[c], recv_sem=ra_sem.at[c],
                        device_id={"gx": p}, device_id_type=MESH).start()
            return 0

        lax.fori_loop(0, tiles_y, tile, 0)
        recv_a[c, pl.ds(my_x, mine_x), :] = send_a[c, :, pl.ds(my_y, mine_y)]
        load_su(c).start()
        return 0

    lax.fori_loop(0, count, first, 0)
    lax.fori_loop(0, tiles_x, build_x, 0)

    def tall_part(ref, c, sem):
        part = ref.at[c, pl.ds(0, size_x - mine_x), :]
        return pltpu.make_async_copy(part, part, sem.at[c])

    def wide_part(ref, c, sem):
        part = ref.at[c, :, pl.ds(0, size_y - mine_y)]
        return pltpu.make_async_copy(part, part, sem.at[c])

    def second(c, _):
        tall_part(recv_a, c, ra_sem).wait()
        hi, lo = parts_of(recv_a[c])
        tall_hi[...] = hi
        tall_lo[...] = lo
        load_su(c).wait()

        def up(t, _):
            out = pl.ds(pl.multiple_of(t * TILE, TILE), TILE)
            recv_a[c, out, :] = send_b[c, out, :] * smooth_x(t)
            return 0

        lax.fori_loop(0, tiles_x, up, 0)
        hi, lo = parts_of(recv_a[c])
        tall_hi[...] = hi
        tall_lo[...] = lo

        def back(s, _):
            t = turn(s, tiles_x, mine_x)
            send_b[c, pl.ds(pl.multiple_of(t * TILE, TILE), TILE), :] = smooth_x(t)
            for k in range(TILE // mine_x):
                p = t * (TILE // mine_x) + k

                @pl.when(p != me)
                def _():
                    pltpu.make_async_remote_copy(
                        src_ref=send_b.at[c, pl.ds(pl.multiple_of(p * mine_x, mine_x), mine_x), :],
                        dst_ref=recv_b.at[c, :, pl.ds(my_y, mine_y)],
                        send_sem=sb_sem.at[c], recv_sem=rb_sem.at[c],
                        device_id={"gx": p}, device_id_type=MESH).start()
            return 0

        lax.fori_loop(0, tiles_x, back, 0)
        recv_b[c, :, pl.ds(my_y, mine_y)] = send_b[c, pl.ds(my_x, mine_x), :]
        return 0

    lax.fori_loop(0, count, second, 0)

    def third(c, _):
        wide_part(send_a, c, sa_sem).wait()
        wide_part(recv_b, c, rb_sem).wait()
        hi, lo = parts_of(recv_b[c])
        wide_hi[...] = hi
        wide_lo[...] = lo

        def tile(t, _):
            smooth_y(c, t)
            return 0

        lax.fori_loop(0, tiles_y, tile, 0)
        return 0

    lax.fori_loop(0, count, third, 0)

    def finish(c, _):
        tall_part(send_b, c, sb_sem).wait()
        return 0

    lax.fori_loop(0, count, finish, 0)


def kernel_form(n, cotangent, saved_v, saved_u, gain_x, width_x, gain_y, width_y):
    count, mine_x, size_y = cotangent.shape
    size_x, mine_y = saved_u.shape[1:]
    rows = jnp.stack([gain_x, width_x.astype(jnp.float32), gain_y, width_y.astype(jnp.float32)])
    f32, bf16 = jnp.float32, jnp.bfloat16
    work = 12 * 2 * count * BAND * (mine_x * size_y + mine_y * size_x)
    return pl.pallas_call(
        functools.partial(fused, n),
        out_shape=(pltpu.VMEM(saved_u.shape, f32), pltpu.VMEM(cotangent.shape, f32)),
        in_specs=[pl.BlockSpec(memory_space=pl.ANY)] * 3 + [pl.BlockSpec(memory_space=pltpu.VMEM)] * 2,
        out_specs=(pl.BlockSpec(memory_space=pltpu.VMEM),) * 2,
        scratch_shapes=[
            pltpu.VMEM((count, size_x, mine_y), f32),
            pltpu.VMEM((count, mine_x, size_y), f32),
            pltpu.VMEM((2, mine_x, size_y), f32),
            pltpu.VMEM((size_y // TILE, BAND, TILE), bf16),
            pltpu.VMEM((size_y // TILE, BAND, TILE), bf16),
            pltpu.VMEM((size_x // TILE, TILE, BAND), bf16),
            pltpu.VMEM((size_x // TILE, TILE, BAND), bf16),
            pltpu.VMEM((mine_x, size_y), bf16),
            pltpu.VMEM((mine_x, size_y), bf16),
            pltpu.VMEM((size_x, mine_y), bf16),
            pltpu.VMEM((size_x, mine_y), bf16),
        ] + [pltpu.SemaphoreType.DMA((count,))] * 7,
        compiler_params=pltpu.CompilerParams(
            collective_id=0, has_side_effects=True, vmem_limit_bytes=44 * 2**20),
        cost_estimate=pl.CostEstimate(
            flops=work, bytes_accessed=20 * cotangent.size, transcendentals=0),
    )(cotangent, saved_v, saved_u, rows, rows.T)


def on_device(n, *arrays):
    size_y, (size_x, mine_y), mine_x = arrays[0].shape[2], arrays[2].shape[1:], arrays[0].shape[1]
    fits = (size_x % (2 * TILE) == 0 and size_y % (2 * TILE) == 0 and min(size_x, size_y) >= BAND
            and mine_x in (128, TILE) and mine_y in (128, TILE) and n > 1)
    return kernel_form(n, *arrays) if fits else plain_form(*arrays)


def solution(mesh):
    in_specs = (
        P("groups", "gx", None),
        P("groups", "gx", None),
        P("groups", None, "gx"),
        P(),
        P(),
        P(),
        P(),
    )
    out_specs = (P("groups", None, "gx"), P("groups", "gx", None))
    return jax.shard_map(
        functools.partial(on_device, mesh.shape["gx"]),
        mesh=mesh, in_specs=in_specs, out_specs=out_specs, check_vma=False
    )
```

```python
import functools
import math

import jax
import jax.numpy as jnp
from jax import lax
from jax.experimental import pallas as pl
from jax.experimental.pallas import tpu as pltpu
from jax.sharding import PartitionSpec as P

SIGMA = 64
REACH = 256
TILE = 256
BAND = TILE + 2 * REACH
SCALE = 1.0 / math.sqrt(SIGMA * math.sqrt(math.pi))
MESH = pl.DeviceIdType.MESH


def build_kernel(gain, width, count):
    rows = jnp.arange(count, dtype=jnp.int32)[:, None]
    cols = jnp.arange(count, dtype=jnp.int32)[None, :]
    offset = (rows - cols).astype(jnp.float32)
    values = gain[:, None] * jnp.exp(-offset * offset / (2.0 * SIGMA * SIGMA)) * SCALE
    cutoff = jnp.minimum(width[:, None], width[None, :])
    return jnp.where(jnp.abs(rows - cols) <= cutoff, values, jnp.zeros_like(values))


def plain_form(cotangent, saved_v, saved_u, gain_x, width_x, gain_y, width_y):
    kernel_x = build_kernel(gain_x, width_x, gain_x.shape[0])
    kernel_y = build_kernel(gain_y, width_y, gain_y.shape[0])
    high = lax.Precision.HIGHEST

    def smooth_x(field):
        return jnp.einsum("ziy,ij->zjy", field, kernel_x, precision=high)

    def smooth_y(field):
        return jnp.einsum("zxi,ij->zxj", field, kernel_y, precision=high)

    weighted = saved_v * cotangent
    along_y = smooth_y(weighted)
    middle = smooth_x(lax.all_to_all(along_y, "gx", split_axis=2, concat_axis=1, tiled=True))
    grad_u = saved_u * middle
    back_x = smooth_x(grad_u)
    grad_v = smooth_y(lax.all_to_all(back_x, "gx", split_axis=1, concat_axis=2, tiled=True))
    return (grad_u, grad_v)


def parts_of(value):
    high = value.astype(jnp.bfloat16)
    return high, (value - high.astype(jnp.float32)).astype(jnp.bfloat16)


def dot(a, b):
    return jnp.dot(a, b, preferred_element_type=jnp.float32)


def three(a_hi, a_lo, b_hi, b_lo):
    return dot(a_hi, b_hi) + dot(a_hi, b_lo) + dot(a_lo, b_hi)


def fused(n, cot, sv, su, gain_x, width_x, gain_y, width_y, recv_a, send_a,
          send_b, recv_b, sv_buf, ky_hi, ky_lo, kx_hi, kx_lo,
          wide_hi, wide_lo, tall_hi, tall_lo,
          cot_sem, sv_sem, su_sem, sa_sem, ra_sem, sb_sem, rb_sem):
    count, mine_x, size_y = cot.shape
    size_x, mine_y = su.shape[1], su.shape[2]
    tiles_x, tiles_y = size_x // TILE, size_y // TILE
    me = lax.axis_index("gx")
    my_x = pl.multiple_of(me * mine_x, mine_x)
    my_y = pl.multiple_of(me * mine_y, mine_y)

    def load_cot(c):
        return pltpu.make_async_copy(cot.at[c], send_a.at[c], cot_sem.at[c])

    def load_sv(c):
        return pltpu.make_async_copy(sv.at[c], sv_buf.at[lax.rem(c, 2)], sv_sem.at[c])

    def load_su(c):
        return pltpu.make_async_copy(su.at[c], send_b.at[c], su_sem.at[c])

    for c in range(count):
        load_cot(c).start()
        if c < 2:
            load_sv(c).start()

    barrier = pltpu.get_barrier_semaphore()
    for k in range(1, n):
        pl.semaphore_signal(barrier, inc=1, device_id={"gx": lax.rem(me + k, n)}, device_id_type=MESH)

    def turn(s, tiles, mine):
        half = tiles // 2
        away = jnp.where(lax.rem(s, 2) == 0, half + s // 2, lax.rem((s + 1) // 2, half))
        return lax.rem(my_tile(mine) + away, tiles)

    def my_tile(mine):
        return me // (TILE // mine)

    def band_start(t, size):
        return pl.multiple_of(jnp.clip(t * TILE - REACH, 0, size - BAND), TILE)

    def values(i, j, gain, width_i, width_j):
        offset = (i - j).astype(jnp.float32)
        cell = gain * jnp.exp(-offset * offset / (2.0 * SIGMA * SIGMA)) * SCALE
        return jnp.where(jnp.abs(offset) <= jnp.minimum(width_i, width_j), cell, 0.0)

    def row(ref, at):
        return ref[:, pl.ds(at, TILE)].astype(jnp.float32)

    def column(ref, at):
        return jnp.broadcast_to(row(ref, at), (128, TILE)).T[:, 0:1]

    def build_y(t, _):
        i0, j0 = band_start(t, size_y), pl.multiple_of(t * TILE, TILE)
        j = j0 + lax.broadcasted_iota(jnp.int32, (TILE, TILE), 1)
        for s in range(BAND // TILE):
            at = pl.multiple_of(i0 + s * TILE, TILE)
            i = at + lax.broadcasted_iota(jnp.int32, (TILE, TILE), 0)
            hi, lo = parts_of(values(i, j, column(gain_y, at), column(width_y, at), row(width_y, j0)))
            ky_hi[t, s * TILE:(s + 1) * TILE, :] = hi
            ky_lo[t, s * TILE:(s + 1) * TILE, :] = lo
        return 0

    def build_x(t, _):
        i0, j0 = band_start(t, size_x), pl.multiple_of(t * TILE, TILE)
        j = j0 + lax.broadcasted_iota(jnp.int32, (TILE, TILE), 0)
        for s in range(BAND // TILE):
            at = pl.multiple_of(i0 + s * TILE, TILE)
            i = at + lax.broadcasted_iota(jnp.int32, (TILE, TILE), 1)
            hi, lo = parts_of(values(i, j, row(gain_x, at), row(width_x, at), column(width_x, j0)))
            kx_hi[t, :, s * TILE:(s + 1) * TILE] = hi
            kx_lo[t, :, s * TILE:(s + 1) * TILE] = lo
        return 0

    def smooth_y(c, t):
        band = pl.ds(band_start(t, size_y), BAND)
        send_a[c, :, pl.ds(pl.multiple_of(t * TILE, TILE), TILE)] = three(
            wide_hi[:, band], wide_lo[:, band], ky_hi[t], ky_lo[t])

    def smooth_x(t):
        band = pl.ds(band_start(t, size_x), BAND)
        return three(kx_hi[t], kx_lo[t], tall_hi[band, :], tall_lo[band, :])

    pl.semaphore_wait(barrier, n - 1)

    def first(c, _):
        load_cot(c).wait()
        load_sv(c).wait()
        hi, lo = parts_of(send_a[c] * sv_buf[lax.rem(c, 2)])
        wide_hi[...] = hi
        wide_lo[...] = lo

        @pl.when(c + 2 < count)
        def _():
            load_sv(c + 2).start()

        def tile(s, _):
            t = turn(s, tiles_y, mine_y)

            @pl.when(c == 0)
            def _():
                build_y(t, 0)

            smooth_y(c, t)
            for k in range(TILE // mine_y):
                p = t * (TILE // mine_y) + k

                @pl.when(p != me)
                def _():
                    pltpu.make_async_remote_copy(
                        src_ref=send_a.at[c, :, pl.ds(pl.multiple_of(p * mine_y, mine_y), mine_y)],
                        dst_ref=recv_a.at[c, pl.ds(my_x, mine_x), :],
                        send_sem=sa_sem.at[c], recv_sem=ra_sem.at[c],
                        device_id={"gx": p}, device_id_type=MESH).start()
            return 0

        lax.fori_loop(0, tiles_y, tile, 0)
        recv_a[c, pl.ds(my_x, mine_x), :] = send_a[c, :, pl.ds(my_y, mine_y)]
        load_su(c).start()
        return 0

    lax.fori_loop(0, count, first, 0)
    lax.fori_loop(0, tiles_x, build_x, 0)

    def tall_part(ref, c, sem):
        part = ref.at[c, pl.ds(0, size_x - mine_x), :]
        return pltpu.make_async_copy(part, part, sem.at[c])

    def wide_part(ref, c, sem):
        part = ref.at[c, :, pl.ds(0, size_y - mine_y)]
        return pltpu.make_async_copy(part, part, sem.at[c])

    def second(c, _):
        tall_part(recv_a, c, ra_sem).wait()
        hi, lo = parts_of(recv_a[c])
        tall_hi[...] = hi
        tall_lo[...] = lo
        load_su(c).wait()

        def up(t, _):
            out = pl.ds(pl.multiple_of(t * TILE, TILE), TILE)
            recv_a[c, out, :] = send_b[c, out, :] * smooth_x(t)
            return 0

        lax.fori_loop(0, tiles_x, up, 0)
        hi, lo = parts_of(recv_a[c])
        tall_hi[...] = hi
        tall_lo[...] = lo

        def back(s, _):
            t = turn(s, tiles_x, mine_x)
            send_b[c, pl.ds(pl.multiple_of(t * TILE, TILE), TILE), :] = smooth_x(t)
            for k in range(TILE // mine_x):
                p = t * (TILE // mine_x) + k

                @pl.when(p != me)
                def _():
                    pltpu.make_async_remote_copy(
                        src_ref=send_b.at[c, pl.ds(pl.multiple_of(p * mine_x, mine_x), mine_x), :],
                        dst_ref=recv_b.at[c, :, pl.ds(my_y, mine_y)],
                        send_sem=sb_sem.at[c], recv_sem=rb_sem.at[c],
                        device_id={"gx": p}, device_id_type=MESH).start()
            return 0

        lax.fori_loop(0, tiles_x, back, 0)
        recv_b[c, :, pl.ds(my_y, mine_y)] = send_b[c, pl.ds(my_x, mine_x), :]
        return 0

    lax.fori_loop(0, count, second, 0)

    def third(c, _):
        wide_part(send_a, c, sa_sem).wait()
        wide_part(recv_b, c, rb_sem).wait()
        hi, lo = parts_of(recv_b[c])
        wide_hi[...] = hi
        wide_lo[...] = lo

        def tile(t, _):
            smooth_y(c, t)
            return 0

        lax.fori_loop(0, tiles_y, tile, 0)
        return 0

    lax.fori_loop(0, count, third, 0)

    def finish(c, _):
        tall_part(send_b, c, sb_sem).wait()
        return 0

    lax.fori_loop(0, count, finish, 0)


def kernel_form(n, cotangent, saved_v, saved_u, gain_x, width_x, gain_y, width_y):
    count, mine_x, size_y = cotangent.shape
    size_x, mine_y = saved_u.shape[1:]
    vectors = [v.reshape(1, -1) for v in (gain_x, width_x, gain_y, width_y)]
    f32, bf16 = jnp.float32, jnp.bfloat16
    work = 12 * 2 * count * BAND * (mine_x * size_y + mine_y * size_x)
    return pl.pallas_call(
        functools.partial(fused, n),
        out_shape=(pltpu.VMEM(saved_u.shape, f32), pltpu.VMEM(cotangent.shape, f32)),
        in_specs=[pl.BlockSpec(memory_space=pl.ANY)] * 3 + [pl.BlockSpec(memory_space=pltpu.VMEM)] * 4,
        out_specs=(pl.BlockSpec(memory_space=pltpu.VMEM),) * 2,
        scratch_shapes=[
            pltpu.VMEM((count, size_x, mine_y), f32),
            pltpu.VMEM((count, mine_x, size_y), f32),
            pltpu.VMEM((2, mine_x, size_y), f32),
            pltpu.VMEM((size_y // TILE, BAND, TILE), bf16),
            pltpu.VMEM((size_y // TILE, BAND, TILE), bf16),
            pltpu.VMEM((size_x // TILE, TILE, BAND), bf16),
            pltpu.VMEM((size_x // TILE, TILE, BAND), bf16),
            pltpu.VMEM((mine_x, size_y), bf16),
            pltpu.VMEM((mine_x, size_y), bf16),
            pltpu.VMEM((size_x, mine_y), bf16),
            pltpu.VMEM((size_x, mine_y), bf16),
        ] + [pltpu.SemaphoreType.DMA((count,))] * 7,
        compiler_params=pltpu.CompilerParams(
            collective_id=0, has_side_effects=True, vmem_limit_bytes=44 * 2**20),
        cost_estimate=pl.CostEstimate(
            flops=work, bytes_accessed=20 * cotangent.size, transcendentals=0),
    )(cotangent, saved_v, saved_u, *vectors)


def on_device(n, *arrays):
    size_y, (size_x, mine_y), mine_x = arrays[0].shape[2], arrays[2].shape[1:], arrays[0].shape[1]
    fits = (size_x % (2 * TILE) == 0 and size_y % (2 * TILE) == 0 and min(size_x, size_y) >= BAND
            and mine_x in (128, TILE) and mine_y in (128, TILE) and n > 1)
    return kernel_form(n, *arrays) if fits else plain_form(*arrays)


def solution(mesh):
    in_specs = (
        P("groups", "gx", None),
        P("groups", "gx", None),
        P("groups", None, "gx"),
        P(),
        P(),
        P(),
        P(),
    )
    out_specs = (P("groups", None, "gx"), P("groups", "gx", None))
    return jax.shard_map(
        functools.partial(on_device, mesh.shape["gx"]),
        mesh=mesh, in_specs=in_specs, out_specs=out_specs, check_vma=False
    )
```
